32 devices in a mesh: gx: 4 (over y, core), gy: 2 (over x), vert: 4 (over z).
Axes of the slice: x: 2, y: 2, z: 4, core: 2. Of those that a mesh axis runs over, the one named last changes fastest.
Arguments:
- recorded: float32 [4, 512, 128, 256], P('vert', 'gx', 'gy'), may hold values from 0.25 to 4
- psf_taps: float32 [4, 3, 31], P('vert'), may hold values from 0.05 to 1
- estimate: float32 [512, 128, 256], P('gx', ('gy', 'vert')), may hold values from 0.5 to 2
Outputs:
- joined: float32 [512, 128, 256], P('gx', ('gy', 'vert'))
The draws below stay inside these ranges and needn't reach their ends.
All inputs are finite; a program needn't handle non-finite values.
Results may differ from the reference program's by a relative error of at most 0.0001.
Values sent between devices are 32-bit elements; how exact they have to be, the bound alone decides.
A program may use at most 128 MiB of HBM per device.

```python
import math
import jax
import jax.numpy as jnp
from jax import lax

Y = 256
TAPS = 31
ITERS = 2
VIEWS = 4
NX = 512
NZ = 128


def block_scale(own_key, shape, cuts, low, high):
    level, own = 1.0, jax.random.fold_in(own_key, 6)
    for dim, parts in cuts:
        draws = jnp.exp(jax.random.uniform(jax.random.fold_in(own, dim), (parts,), jnp.float32, low / len(cuts), high / len(cuts)))
        level = level * jnp.repeat(draws, shape[dim] // parts).reshape([-1 if axis == dim else 1 for axis in range(len(shape))])
    return level


def setup_inputs(seed: int = 0) -> dict:
    key_list = jax.random.split(jax.random.key(seed), 4)
    return {
        "recorded": jnp.clip(jnp.exp(math.log(4.0) - 2.7725887 * jax.random.uniform(key_list[0], (VIEWS, NX, NZ, Y), jnp.float32) ** block_scale(key_list[0], (VIEWS, NX, NZ, Y), ((0, 4), (1, 4), (2, 2)), -0.2, 0.2)), 0.25, 4.0),
        "psf_taps": jnp.clip(jnp.exp(math.log(1.0) - 2.9957323 * jax.random.uniform(key_list[1], (VIEWS, 3, TAPS), jnp.float32) ** block_scale(key_list[1], (VIEWS, 3, TAPS), ((0, 4),), -0.2, 0.2)), 0.05, 1.0),
        "estimate": jnp.clip(jnp.exp(math.log(2.0) - 1.3862944 * jax.random.uniform(key_list[2], (NX, NZ, Y), jnp.float32) ** block_scale(key_list[2], (NX, NZ, Y), ((0, 4), (1, 8)), -0.2, 0.2)), 0.5, 2.0),
    }


def band(kernel, out_size, in_size, shift_cells, adjoint):
    half_width = (kernel.shape[0] - 1) // 2
    out_index = lax.broadcasted_iota(jnp.int32, (out_size, in_size), 0)
    in_index = lax.broadcasted_iota(jnp.int32, (out_size, in_size), 1)
    offset_cells = in_index - out_index + shift_cells
    if adjoint:
        tap_index = half_width + offset_cells
    else:
        tap_index = half_width - offset_cells
    choose = tap_index[:, :, None] == lax.broadcasted_iota(jnp.int32, (1, 1, kernel.shape[0]), 2)
    return jnp.sum(jnp.where(choose, kernel, jnp.zeros_like(kernel)), axis=2)


def blur_block(volume, kernels, out_x, out_y, shift_cells, adjoint):
    depth_cells = volume.shape[2]
    highest = lax.Precision.HIGHEST
    x_matrix = band(kernels[0], out_x, volume.shape[0], shift_cells, adjoint)
    y_matrix = band(kernels[1], out_y, volume.shape[1], shift_cells, adjoint)
    z_matrix = band(kernels[2], depth_cells, depth_cells, 0, adjoint)
    result = jnp.einsum("pi,ijk->pjk", x_matrix, volume, precision=highest)
    result = jnp.einsum("qj,pjk->pqk", y_matrix, result, precision=highest)
    return jnp.einsum("pqk,rk->pqr", result, z_matrix, precision=highest)


def reference(recorded, psf_taps, estimate):
    kernels_all = psf_taps / jnp.sum(psf_taps, axis=2, keepdims=True)
    joined = estimate
    size_x = estimate.shape[0]
    size_y = estimate.shape[1]
    for iteration in range(ITERS):
        def add_view(summed, view_pair):
            view_data, kernels = view_pair
            blurred = blur_block(joined, kernels, size_x, size_y, 0, False)
            ratio = view_data / blurred
            return summed + blur_block(ratio, kernels, size_x, size_y, 0, True), None

        summed, unused = lax.scan(add_view, jnp.zeros_like(estimate), (recorded, kernels_all))
        joined = joined * (summed / VIEWS)
    return joined
```

```python
import jax
import jax.numpy as jnp
from jax import lax
from jax.sharding import PartitionSpec as P

ITERS = 2
PIECES = 2


def halo(x, axis, dim, width):
    size, length = (lax.axis_size(axis), x.shape[dim])
    up = [(i, i + 1) for i in range(size - 1)]
    down = [(i + 1, i) for i in range(size - 1)]
    before = lax.ppermute(lax.slice_in_dim(x, length - width, length, axis=dim), axis, up)
    after = lax.ppermute(lax.slice_in_dim(x, 0, width, axis=dim), axis, down)
    return before, after


def band(kernel, out_size, in_size, shift_cells, adjoint):
    half_width = (kernel.shape[0] - 1) // 2
    out_index = lax.broadcasted_iota(jnp.int32, (out_size, in_size), 0)
    in_index = lax.broadcasted_iota(jnp.int32, (out_size, in_size), 1)
    offset_cells = in_index - out_index + shift_cells
    if adjoint:
        tap_index = half_width + offset_cells
    else:
        tap_index = half_width - offset_cells
    choose = tap_index[:, :, None] == lax.broadcasted_iota(jnp.int32, (1, 1, kernel.shape[0]), 2)
    return jnp.sum(jnp.where(choose, kernel, jnp.zeros_like(kernel)), axis=2)


def body(recorded, psf_taps, estimate):
    m = (psf_taps.shape[2] - 1) // 2
    view_count = psf_taps.shape[0] * lax.axis_size("vert")
    kernels = psf_taps[0] / jnp.sum(psf_taps[0], axis=1, keepdims=True)
    view_data = recorded[0]
    bx, bz, by = view_data.shape
    rows = bx // PIECES
    high = lax.Precision.HIGH
    mats = []
    for adjoint in (False, True):
        mats.append((
            band(kernels[0], bx, bx + 2 * m, -m, adjoint),
            band(kernels[1], bz, bz + 2 * m, -m, adjoint),
            band(kernels[2], by, by, 0, adjoint),
        ))
    order = []
    for i in range((PIECES + 1) // 2):
        order += [i] if i == PIECES - 1 - i else [i, PIECES - 1 - i]

    def dims12(piece, zmat, ymat):
        before, after = halo(piece, "gy", 1, m)
        wide = jnp.concatenate([before, piece, after], axis=1)
        out = jnp.einsum("qj,pjk->pqk", zmat, wide, precision=high)
        return jnp.einsum("pqk,rk->pqr", out, ymat, precision=high)

    own = [estimate[i * rows:(i + 1) * rows] for i in range(PIECES)]
    for iteration in range(ITERS):
        fx, fz, fy = mats[0]
        blur = [None] * PIECES
        last = None
        for i in order:
            src = own[i]
            if last is not None:
                src, last = lax.optimization_barrier((src, last))
            last = lax.all_gather(src, "vert", axis=1, tiled=True)
            blur[i] = last
        blur = [dims12(b, fz, fy) for b in blur]
        nx_before, nx_after = edge_halo(blur, m)
        wide = jnp.concatenate([nx_before] + blur + [nx_after], axis=0)
        blurred = jnp.einsum("pi,ijk->pjk", fx, wide, precision=high)
        ratio = view_data / blurred
        ax, az, ay = mats[1]
        before, after = halo(ratio, "gx", 0, m)
        wide = jnp.concatenate([before, ratio, after], axis=0)
        new = [None] * PIECES
        last = None
        for i in order:
            lo = i * rows
            part = jnp.einsum("pi,ijk->pjk", ax[lo:lo + rows, lo:lo + rows + 2 * m], wide[lo:lo + rows + 2 * m], precision=high)
            corr = dims12(part, az, ay)
            if last is not None:
                corr, last = lax.optimization_barrier((corr, last))
            last = lax.psum_scatter(corr, "vert", scatter_dimension=1, tiled=True)
            new[i] = own[i] * (last / view_count)
        own = new
    return jnp.concatenate(own, axis=0)


def edge_halo(parts, m):
    size = lax.axis_size("gx")
    before = lax.ppermute(parts[-1][-m:], "gx", [(i, i + 1) for i in range(size - 1)])
    after = lax.ppermute(parts[0][:m], "gx", [(i + 1, i) for i in range(size - 1)])
    return before, after


def solution(mesh):
    in_specs = (P("vert", "gx", "gy", None), P("vert", None, None), P("gx", ("gy", "vert"), None))
    out_specs = P("gx", ("gy", "vert"), None)
    return jax.shard_map(body, mesh=mesh, in_specs=in_specs, out_specs=out_specs, check_vma=False)
```

```python
import jax
import jax.numpy as jnp
from jax import lax
from jax.sharding import PartitionSpec as P

ITERS = 2


def swap(last, first, axis):
    size = lax.axis_size(axis)
    before = lax.ppermute(last, axis, [(i, i + 1) for i in range(size - 1)])
    behind = lax.ppermute(first, axis, [(i + 1, i) for i in range(size - 1)])
    return before, behind


def band(kernel, out_size, in_size, shift_cells, adjoint):
    half_width = (kernel.shape[0] - 1) // 2
    out_index = lax.broadcasted_iota(jnp.int32, (out_size, in_size), 0)
    in_index = lax.broadcasted_iota(jnp.int32, (out_size, in_size), 1)
    offset_cells = in_index - out_index + shift_cells
    if adjoint:
        tap_index = half_width + offset_cells
    else:
        tap_index = half_width - offset_cells
    choose = tap_index[:, :, None] == lax.broadcasted_iota(jnp.int32, (1, 1, kernel.shape[0]), 2)
    return jnp.sum(jnp.where(choose, kernel, jnp.zeros_like(kernel)), axis=2)


def after(x, done):
    return x + 0.0 * done[0, 0, 0]


def body(recorded, psf_taps, estimate):
    m = (psf_taps.shape[2] - 1) // 2
    view_count = psf_taps.shape[0] * lax.axis_size("vert")
    kernels = psf_taps[0] / jnp.sum(psf_taps[0], axis=1, keepdims=True)
    view_data = recorded[0]
    bx, bz, by = view_data.shape
    e = bx // 4
    high = lax.Precision.HIGH
    mats = []
    for adjoint in (False, True):
        mats.append((
            band(kernels[0], bx, bx + 2 * m, -m, adjoint),
            band(kernels[1], bz, bz + 2 * m, -m, adjoint),
            band(kernels[2], by, by, 0, adjoint),
        ))
    (fx, fz, fy), (ax, az, ay) = mats

    def dims12(piece, zmat, ymat, done=None):
        length = piece.shape[1]
        low, high_rows = piece[:, :m], piece[:, length - m:]
        if done is not None:
            low, high_rows = after(low, done), after(high_rows, done)
        before, behind = swap(high_rows, low, "gy")
        wide = jnp.concatenate([before, piece, behind], axis=1)
        out = jnp.einsum("qj,pjk->pqk", zmat, wide, precision=high)
        return jnp.einsum("pqk,rk->pqr", out, ymat, precision=high)

    def along_x(mat, wide):
        return jnp.einsum("pi,ijk->pjk", mat, wide, precision=high)

    def gather(x):
        return lax.all_gather(x, "vert", axis=1, tiled=True)

    def scatter(x):
        return lax.psum_scatter(x, "vert", scatter_dimension=1, tiled=True)

    own_edge = jnp.concatenate([estimate[:e], estimate[bx - e:]], axis=0)
    own_mid = estimate[e:bx - e]
    for iteration in range(ITERS):
        edge = gather(own_edge)
        own_mid, edge = lax.optimization_barrier((own_mid, edge))
        mid = gather(own_mid)
        edge = dims12(edge, fz, fy)
        before, behind = swap(edge[2 * e - m:], edge[:m], "gx")
        mid = dims12(mid, fz, fy, edge)
        wide = jnp.concatenate([before, edge[:e], mid, edge[e:], behind], axis=0)
        ratio = view_data / along_x(fx, wide)
        part = along_x(ax[e:bx - e, e:bx - e + 2 * m], ratio[e - m:bx - e + m])
        corr_mid = dims12(part, az, ay)
        sum_mid = scatter(corr_mid)
        before, behind = swap(after(ratio[bx - m:], corr_mid), after(ratio[:m], corr_mid), "gx")
        low = jnp.concatenate([before, ratio[:e + m]], axis=0)
        upper = jnp.concatenate([ratio[bx - e - m:], behind], axis=0)
        part = jnp.concatenate([
            along_x(ax[:e, :e + 2 * m], low),
            along_x(ax[bx - e:, bx - e:], upper),
        ], axis=0)
        corr_edge = dims12(part, az, ay)
        sum_edge = scatter(corr_edge)
        own_mid = own_mid * (sum_mid / view_count)
        own_edge = own_edge * (sum_edge / view_count)
    return jnp.concatenate([own_edge[:e], own_mid, own_edge[e:]], axis=0)


def solution(mesh):
    in_specs = (P("vert", "gx", "gy", None), P("vert", None, None), P("gx", ("gy", "vert"), None))
    out_specs = P("gx", ("gy", "vert"), None)
    return jax.shard_map(body, mesh=mesh, in_specs=in_specs, out_specs=out_specs, check_vma=False)
```

```python
import jax
import jax.numpy as jnp
from jax import lax
from jax.sharding import PartitionSpec as P

ITERS = 2


def swap(last, first, axis):
    size = lax.axis_size(axis)
    before = lax.ppermute(last, axis, [(i, i + 1) for i in range(size - 1)])
    behind = lax.ppermute(first, axis, [(i + 1, i) for i in range(size - 1)])
    return before, behind


def band(kernel, out_size, in_size, shift_cells, adjoint):
    half_width = (kernel.shape[0] - 1) // 2
    out_index = lax.broadcasted_iota(jnp.int32, (out_size, in_size), 0)
    in_index = lax.broadcasted_iota(jnp.int32, (out_size, in_size), 1)
    offset_cells = in_index - out_index + shift_cells
    if adjoint:
        tap_index = half_width + offset_cells
    else:
        tap_index = half_width - offset_cells
    choose = tap_index[:, :, None] == lax.broadcasted_iota(jnp.int32, (1, 1, kernel.shape[0]), 2)
    return jnp.sum(jnp.where(choose, kernel, jnp.zeros_like(kernel)), axis=2)


def after(x, done):
    return x + 0.0 * done[0, 0, 0]


def body(recorded, psf_taps, estimate):
    m = (psf_taps.shape[2] - 1) // 2
    view_count = psf_taps.shape[0] * lax.axis_size("vert")
    kernels = psf_taps[0] / jnp.sum(psf_taps[0], axis=1, keepdims=True)
    view_data = recorded[0]
    bx, bz, by = view_data.shape
    e = bx // 4
    high = lax.Precision.HIGH
    mats = []
    for adjoint in (False, True):
        mats.append((
            band(kernels[0], bx, bx + 2 * m, -m, adjoint),
            band(kernels[1], bz, bz + 2 * m, -m, adjoint),
            band(kernels[2], by, by, 0, adjoint),
        ))
    (fx, fz, fy), (ax, az, ay) = mats
    h = -(-m // 8) * 8
    fx = band(kernels[0], bx, bx + 2 * h, -h, False)
    fx = jnp.concatenate([
        fx[:, h:h + e], fx[:, h + bx - e:h + bx], fx[:, h + e:h + bx - e], fx[:, :h], fx[:, h + bx:],
    ], axis=1)

    def dims12(piece, zmat, ymat, done=None):
        length = piece.shape[1]
        low, high_rows = piece[:, :m], piece[:, length - m:]
        if done is not None:
            low, high_rows = after(low, done), after(high_rows, done)
        before, behind = swap(high_rows, low, "gy")
        wide = jnp.concatenate([before, piece, behind], axis=1)
        out = jnp.einsum("qj,pjk->pqk", zmat, wide, precision=high)
        return jnp.einsum("pqk,rk->pqr", out, ymat, precision=high)

    def along_x(mat, wide):
        return jnp.einsum("pi,ijk->pjk", mat, wide, precision=high)

    def gather(x):
        return lax.all_gather(x, "vert", axis=1, tiled=True)

    def scatter(x):
        return lax.psum_scatter(x, "vert", scatter_dimension=1, tiled=True)

    own_edge = jnp.concatenate([estimate[:e], estimate[bx - e:]], axis=0)
    own_mid = estimate[e:bx - e]
    for iteration in range(ITERS):
        edge = gather(own_edge)
        own_mid, edge = lax.optimization_barrier((own_mid, edge))
        mid = gather(own_mid)
        edge = dims12(edge, fz, fy)
        before, behind = swap(edge[2 * e - h:], edge[:h], "gx")
        mid = dims12(mid, fz, fy, edge)
        wide = jnp.concatenate([edge, mid, before, behind], axis=0)
        ratio = view_data / along_x(fx, wide)
        part = along_x(ax[e:bx - e, e:bx - e + 2 * m], ratio[e - m:bx - e + m])
        corr_mid = dims12(part, az, ay)
        sum_mid = scatter(corr_mid)
        before, behind = swap(after(ratio[bx - m:], corr_mid), after(ratio[:m], corr_mid), "gx")
        low = jnp.concatenate([before, ratio[:e + m]], axis=0)
        upper = jnp.concatenate([ratio[bx - e - m:], behind], axis=0)
        part = jnp.concatenate([
            along_x(ax[:e, :e + 2 * m], low),
            along_x(ax[bx - e:, bx - e:], upper),
        ], axis=0)
        corr_edge = dims12(part, az, ay)
        sum_mid, corr_edge = lax.optimization_barrier((sum_mid, corr_edge))
        sum_edge = scatter(corr_edge)
        own_mid = own_mid * (sum_mid / view_count)
        own_edge = own_edge * (sum_edge / view_count)
    return jnp.concatenate([own_edge[:e], own_mid, own_edge[e:]], axis=0)


def solution(mesh):
    in_specs = (P("vert", "gx", "gy", None), P("vert", None, None), P("gx", ("gy", "vert"), None))
    out_specs = P("gx", ("gy", "vert"), None)
    return jax.shard_map(body, mesh=mesh, in_specs=in_specs, out_specs=out_specs, check_vma=False)
```
